32 devices in a mesh: patch: 8 (over z, y), fsdp: 4 (over x, core).
Axes of the slice: x: 2, y: 2, z: 4, core: 2. Of those that a mesh axis runs over, the one named last changes fastest.
Arguments:
- observed: bfloat16 [16384, 256], P(('patch', 'fsdp')), may hold values from -6 to 6
- route: int32 [16384, 1], P(('patch', 'fsdp')), may hold values from 0 to 7, as said below
- grid: bfloat16 [4096, 2048], P(('patch', 'fsdp'))
- gain: float32 [2048], replicated, may hold values from 0.5 to 1.5
- query_weight: bfloat16 [2048, 2048], P(None, 'fsdp'), may hold values from -0.125 to 0.125
- key_weight: bfloat16 [256, 2048], replicated, may hold values from -1 to 1
- value_weight: bfloat16 [256, 2048], replicated, may hold values from -0.375 to 0.375
- up_weight: bfloat16 [2048, 4096], P(None, 'fsdp'), may hold values from -0.125 to 0.125
- down_weight: bfloat16 [4096, 2048], P('fsdp'), may hold values from -0.09375 to 0.09375
- cotangent: bfloat16 [4096, 2048], P(('patch', 'fsdp')), may hold values from -6 to 6
Outputs:
- layer_output: bfloat16 [4096, 2048], P(('patch', 'fsdp'))
- input_grad: bfloat16 [4096, 2048], P(('patch', 'fsdp'))
- up_grad: float32 [2048, 4096], P('patch', 'fsdp')
- down_grad: float32 [4096, 2048], P('fsdp', 'patch')
The draws below stay inside these ranges and needn't reach their ends.
Inputs may be any that keep to these rules, and one draw needn't show every extreme that they name: `route`: within the rows of one device (aligned blocks of 512 rows) no patch is named by more than 128 rows, and in every block some patch is named by exactly 128.
All inputs are finite; a program needn't handle non-finite values.
Results may differ from the reference program's by a relative error of at most 0.013.
Values may be sent and summed in bfloat16 or wider, within the bound.
A program may use at most 192 MiB of HBM per device.

```python
import jax
import jax.numpy as jnp
from jax import lax

D = 2048
C = 256
HEADS = 16
FFW = 4096
DEVICE_TOKENS = 128
OBS_DEV = 512
CAP = 128
TOKENS = 4096
OBS = 16384
N_PATCH = 8
N_FSDP = 4
DEVICES = 32


def draw_grid(key, part):
    key = jax.random.fold_in(key, 7)
    return jax.random.normal(key, (TOKENS, D), jnp.float32).astype(jnp.bfloat16)


def draw_route(key, part):
    key = jax.random.fold_in(key, 11)
    sparse_key, weight_key, block_pick, full_key, block_key = jax.random.split(key, 5)
    regular_count = N_PATCH - 2
    patch_ids = jnp.arange(N_PATCH, dtype=jnp.int32)
    sparse_ids = (1 + jax.random.permutation(sparse_key, regular_count)[:2]).astype(jnp.int32)
    is_sparse = (patch_ids == sparse_ids[0]) | (patch_ids == sparse_ids[1])
    regular = jnp.argsort(is_sparse.astype(jnp.int32)).astype(jnp.int32)
    weights = jnp.power(2, jax.random.randint(weight_key, (N_PATCH,), 0, 5)).astype(jnp.int32)
    full_patch = regular[jax.random.randint(full_key, (), 0, regular_count)]
    rare_blocks = jax.random.permutation(block_pick, DEVICES).astype(jnp.int32) < 2
    least_cap = (CAP * N_PATCH + 2 * regular_count - 1) // (2 * regular_count)
    positions = jnp.arange(OBS_DEV, dtype=jnp.int32)

    def one_block(block_index):
        block_rng = jax.random.fold_in(block_key, block_index)
        cap_key, order_key, shuffle_key = jax.random.split(block_rng, 3)
        leading = regular[block_index % regular_count]
        forced = (patch_ids == full_patch) | (patch_ids == leading)
        drawn_caps = jax.random.randint(cap_key, (N_PATCH,), least_cap, CAP + 1)
        capacity = jnp.where(is_sparse, 0, jnp.where(forced, CAP, drawn_caps)).astype(jnp.int32)
        random_rank = jax.random.randint(order_key, (N_PATCH,), 0, 4096) * weights * N_PATCH + patch_ids
        priority = jnp.where(patch_ids == full_patch, 1 << 29, jnp.where(patch_ids == leading, 1 << 28, random_rank))
        priority = jnp.where(is_sparse, -1 - patch_ids, priority).astype(jnp.int32)
        ranking = jnp.argsort(-priority).astype(jnp.int32)
        filled = jnp.cumsum(capacity[ranking])
        rare_row = rare_blocks[block_index].astype(jnp.int32)
        remaining = OBS_DEV - rare_row
        position_slot = jnp.sum((filled[None, :] <= positions[:, None]).astype(jnp.int32), axis=1)
        position_slot = jnp.minimum(position_slot, N_PATCH - 1)
        assigned = jnp.where(positions < remaining, ranking[position_slot], sparse_ids[1])
        return assigned[jax.random.permutation(shuffle_key, OBS_DEV)]
    blocks = lax.map(one_block, jnp.arange(DEVICES, dtype=jnp.int32))
    return blocks.reshape(OBS_DEV * DEVICES, 1).astype(jnp.int32)


def block_levels(rng, dims, pieces, least, largest):
    factor_of = 1.0
    for position, blocks in pieces:
        draws = jax.random.uniform(jax.random.fold_in(jax.random.fold_in(rng, 6), position), (blocks,), jnp.float32, least / len(pieces), largest / len(pieces))
        factor_of = factor_of * jnp.repeat(jnp.exp(draws), dims[position] // blocks).reshape((-1,) + (1,) * (len(dims) - 1 - position))
    return factor_of


def centred(own_key, extent, deviation, reach, cuts=(), held_as=jnp.bfloat16):
    entries = jax.random.normal(own_key, extent, jnp.float32) * deviation
    if len(cuts) > 0:
        entries = block_levels(own_key, extent, cuts, -0.22, 0.18) * entries
    return jnp.clip(entries, min=-reach, max=reach).astype(held_as)


def setup_inputs(seed: int = 0) -> dict:
    seeds = jax.random.split(jax.random.key(seed), 11)
    observed = centred(seeds[0], (OBS, C), 1.0, 6.0, ((0, 32),))
    route = draw_route(jax.random.fold_in(seeds[10], 71), 0)
    grid = draw_grid(jax.random.fold_in(seeds[10], 71), 0)
    gain = jnp.clip(1.0 + 0.1 * jax.random.normal(seeds[3], (D,), jnp.float32), 0.5, 1.5)
    query_weight = centred(seeds[4], (D, D), D ** -0.5, 0.125, ((1, 4),))
    key_weight = centred(seeds[5], (C, D), (C // 9) ** -0.5, 1.0)
    value_weight = centred(seeds[6], (C, D), C ** -0.5, 0.375)
    up_weight = centred(seeds[7], (D, FFW), D ** -0.5, 0.125, ((1, 4),))
    down_weight = centred(seeds[8], (FFW, D), FFW ** -0.5, 0.09375, ((0, 4),))
    cotangent = centred(seeds[9], (TOKENS, D), 1.0, 6.0, ((0, 32),))
    return {"observed": observed, "route": route, "grid": grid, "gain": gain, "query_weight": query_weight, "key_weight": key_weight, "value_weight": value_weight, "up_weight": up_weight, "down_weight": down_weight, "cotangent": cotangent}


eps = 1e-05

def gelu_tanh(values):
    return jax.nn.gelu(values, approximate=True)

def reference(observed, route, grid, gain, query_weight, key_weight, value_weight, up_weight, down_weight, cotangent):
    group_rows = DEVICE_TOKENS * N_FSDP
    head_width = D // HEADS
    key_limit = N_PATCH * N_FSDP * CAP
    scaling = 1.0 / head_width ** 0.5
    targets = route[:, 0]

    def one_patch(patch_id):
        start_row = (patch_id * group_rows).astype(jnp.int32)
        rows_q = lax.dynamic_slice_in_dim(grid, start_row, group_rows, 0)
        queries = jnp.dot(rows_q, query_weight, preferred_element_type=jnp.float32).astype(jnp.bfloat16)
        queries = queries.reshape(group_rows, HEADS, head_width)
        belongs = targets == patch_id
        counted = jnp.sum(belongs.astype(jnp.int32))
        picked = jnp.nonzero(belongs, size=key_limit, fill_value=0)[0].astype(jnp.int32)
        chosen = observed[picked]
        key_rows = jnp.dot(chosen, key_weight, preferred_element_type=jnp.float32).astype(jnp.bfloat16)
        key_rows = key_rows.reshape(key_limit, HEADS, head_width)
        value_rows = jnp.dot(chosen, value_weight, preferred_element_type=jnp.float32).astype(jnp.bfloat16)
        value_rows = value_rows.reshape(key_limit, HEADS, head_width)
        is_live = jnp.arange(key_limit, dtype=jnp.int32) < counted
        scores = jnp.einsum('thd,khd->thk', queries.astype(jnp.float32), key_rows.astype(jnp.float32)) * scaling
        scores = jnp.where(is_live[None, None, :], scores, -1e+30)
        rowmax = jnp.maximum(lax.optimization_barrier(jnp.max(scores, axis=-1)), 0.0)
        lifted = jnp.exp(scores - rowmax[..., None])
        denominator = jnp.exp(-rowmax) + lax.optimization_barrier(jnp.sum(lifted, axis=-1))
        weights = lifted.astype(jnp.bfloat16)
        blended = jnp.einsum('thk,khd->thd', weights.astype(jnp.float32), value_rows.astype(jnp.float32))
        return (blended / denominator[..., None]).reshape(group_rows, D)
    attention = lax.map(one_patch, jnp.arange(N_PATCH, dtype=jnp.int32)).reshape(TOKENS, D)
    assimilated = (grid.astype(jnp.float32) + attention).astype(jnp.bfloat16)
    values32 = assimilated.astype(jnp.float32)
    mean_removed = values32 - lax.optimization_barrier(jnp.mean(values32, axis=-1, keepdims=True))
    inverse_stddev = lax.rsqrt(lax.optimization_barrier(jnp.mean(mean_removed * mean_removed, axis=-1, keepdims=True)) + eps)
    standardized_input = mean_removed * inverse_stddev
    layer_normed_rows = (standardized_input * gain).astype(jnp.bfloat16)
    pre = jnp.dot(layer_normed_rows, up_weight, preferred_element_type=jnp.float32)
    hidden = gelu_tanh(pre).astype(jnp.bfloat16)
    branch = jnp.dot(hidden, down_weight, preferred_element_type=jnp.float32)
    layer_output = (values32 + branch).astype(jnp.bfloat16)
    back_hidden = jnp.dot(cotangent, down_weight.T, preferred_element_type=jnp.float32)
    slope = jax.vjp(gelu_tanh, pre)[1](back_hidden)[0]
    pre_grad = slope.astype(jnp.bfloat16)
    normed_grad = jnp.dot(pre_grad, up_weight.T, preferred_element_type=jnp.float32)
    gain_scaled = normed_grad * gain
    input_gradient = inverse_stddev * (gain_scaled - lax.optimization_barrier(jnp.mean(gain_scaled, axis=-1, keepdims=True)) - standardized_input * lax.optimization_barrier(jnp.mean(gain_scaled * standardized_input, axis=-1, keepdims=True)))
    input_grad = (cotangent.astype(jnp.float32) + input_gradient).astype(jnp.bfloat16)
    up_grad = jnp.dot(layer_normed_rows.T, pre_grad, preferred_element_type=jnp.float32)
    down_grad = jnp.dot(hidden.T, cotangent, preferred_element_type=jnp.float32)
    return (layer_output, input_grad, up_grad, down_grad)
```

```python
import jax
import jax.numpy as jnp
from jax import lax
from jax.experimental import pallas as pl
from jax.experimental.pallas import tpu as pltpu
from jax.sharding import PartitionSpec as P

D = 2048
HEADS = 16


eps = 1e-05


def gelu_tanh(values):
    return jax.nn.gelu(values, approximate=True)


def pack_rows(observed, route, patches, capacity):
    targets = route[:, 0]
    onehot = (targets[:, None] == jnp.arange(patches, dtype=jnp.int32)[None, :]).astype(jnp.int32)
    ranks = jnp.sum(onehot * (jnp.cumsum(onehot, axis=0) - 1), axis=1)
    slots = targets * capacity + ranks
    packed = (
        jnp.zeros((patches * capacity, observed.shape[1]), observed.dtype).at[slots].set(observed)
    )
    counts = jnp.sum(onehot, axis=0)
    return (packed.reshape(patches, capacity, observed.shape[1]), counts)


def attention_kernel(q_ref, obs_ref, live_ref, wk_ref, wv_ref, grid_ref, out_ref, k_ref, v_ref, s_ref):
    keys, width = k_ref.shape
    block = min(1024, keys)
    rows = s_ref.shape[0]
    scale = 1.4426950408889634 / width**0.5

    @pl.when(pl.program_id(0) == 0)
    def _():
        v_ref[:, width:] = live_ref[...]

    for start in range(0, keys, block):
        piece = obs_ref[start : start + block, :]
        k_ref[start : start + block, :] = jnp.dot(
            piece, wk_ref[...], preferred_element_type=jnp.float32
        ).astype(jnp.bfloat16)
        v_ref[start : start + block, :width] = jnp.dot(
            piece, wv_ref[...], preferred_element_type=jnp.float32
        ).astype(jnp.bfloat16)

    @pl.loop(0, q_ref.shape[0] // rows)
    def _(index):
        here = pl.ds(pl.multiple_of(index * rows, rows), rows)
        queries = q_ref[here, :]
        peak = jnp.zeros((rows, 128), jnp.float32)
        for start in range(0, keys, block):
            scores = lax.dot_general(
                queries,
                k_ref[start : start + block, :],
                (((1,), (1,)), ((), ())),
                preferred_element_type=jnp.float32,
            )
            s_ref[:, start : start + block] = scores
            for lane in range(0, block, 128):
                peak = jnp.maximum(peak, scores[:, lane : lane + 128])
        rowmax = jnp.max(peak, axis=-1, keepdims=True)
        total = jnp.zeros((rows, 2 * width), jnp.float32)
        for start in range(0, keys, block):
            lifted = jnp.exp2((s_ref[:, start : start + block] - rowmax) * scale)
            total = total + jnp.dot(
                lifted.astype(jnp.bfloat16),
                v_ref[start : start + block, :],
                preferred_element_type=jnp.float32,
            )
        denominator = total[:, width:] + jnp.exp2(-rowmax * scale)
        attended = total[:, :width] / denominator
        out_ref[here, :] = (grid_ref[here, :].astype(jnp.float32) + attended).astype(jnp.bfloat16)


def attend(queries, obs_rows, live, key_cols, value_cols, grid_cols, head_width):
    tokens, columns = queries.shape
    keys, channels = obs_rows.shape
    rows = min(256, tokens)
    by_head = lambda length: pl.BlockSpec((length, head_width), lambda h: (0, h))
    whole = lambda shape: pl.BlockSpec(shape, lambda h: (0, 0))
    return pl.pallas_call(
        attention_kernel,
        grid=(columns // head_width,),
        in_specs=[
            by_head(tokens),
            whole((keys, channels)),
            whole((keys, head_width)),
            by_head(channels),
            by_head(channels),
            by_head(tokens),
        ],
        out_specs=by_head(tokens),
        out_shape=jax.ShapeDtypeStruct((tokens, columns), jnp.bfloat16),
        scratch_shapes=[
            pltpu.VMEM((keys, head_width), jnp.bfloat16),
            pltpu.VMEM((keys, 2 * head_width), jnp.bfloat16),
            pltpu.VMEM((rows, keys), jnp.float32),
        ],
        compiler_params=pltpu.CompilerParams(vmem_limit_bytes=48 * 1024 * 1024),
        cost_estimate=pl.CostEstimate(
            flops=4 * tokens * keys * columns * 2, bytes_accessed=keys * channels * 4, transcendentals=tokens * keys * 4
        ),
    )(queries, obs_rows, live, key_cols, value_cols, grid_cols)


def pick(parts, index):
    return lax.dynamic_index_in_dim(parts, index, 0, keepdims=False)


def add(first, second):
    return (first.astype(jnp.float32) + second.astype(jnp.float32)).astype(jnp.bfloat16)


def line_scatter(parts, place, length):
    right = left = None
    for step in range(length - 1):
        send = pick(parts, jnp.clip(length - 1 - step + place, 0, length - 1))
        right = lax.ppermute(
            send if right is None else add(send, right),
            "patch",
            [(2 * a + y, 2 * a + 2 + y) for a in range(step + 1) for y in range(2)],
        )
        send = pick(parts, jnp.clip(step - (length - 1) + place, 0, length - 1))
        left = lax.ppermute(
            send if left is None else add(send, left),
            "patch",
            [(2 * a + y, 2 * a - 2 + y) for a in range(length - 1 - step, length) for y in range(2)],
        )
    total = pick(parts, place).astype(jnp.float32)
    return total if right is None else total + right.astype(jnp.float32) + left.astype(jnp.float32)


def swap_pairs(patches):
    return [(p, p ^ 1) for p in range(patches)]


def scatter_pair_first(partial, patches):
    length = patches // 2
    patch = lax.axis_index("patch")
    place, side = patch // 2, patch % 2
    blocks = partial.reshape(length, 2, -1, partial.shape[1])
    mine = lax.dynamic_index_in_dim(blocks, side, 1, keepdims=False)
    theirs = lax.dynamic_index_in_dim(blocks, 1 - side, 1, keepdims=False)
    return line_scatter(add(mine, lax.ppermute(theirs, "patch", swap_pairs(patches))), place, length)


def scatter_line_first(partial, patches):
    length = patches // 2
    patch = lax.axis_index("patch")
    place, side = patch // 2, patch % 2
    blocks = partial.reshape(length, 2, -1, partial.shape[1])
    pair = line_scatter(blocks, place, length)
    got = lax.ppermute(pick(pair, 1 - side).astype(jnp.bfloat16), "patch", swap_pairs(patches))
    return pick(pair, side) + got.astype(jnp.float32)


def on_device(
    observed,
    route,
    grid,
    gain,
    query_weight,
    key_weight,
    value_weight,
    up_weight,
    down_weight,
    cotangent,
):
    patches = lax.axis_size("patch")
    groups = lax.axis_size("fsdp")
    place = lax.axis_index("fsdp")
    token_count = grid.shape[0]
    head_width = D // HEADS
    columns = query_weight.shape[1]
    capacity = 2 * observed.shape[0] // patches
    all_grid = lax.all_gather(grid, "fsdp", axis=0, tiled=True)
    packed, counts = pack_rows(observed, route, patches, capacity)
    packed = lax.all_to_all(packed, "patch", split_axis=0, concat_axis=0, tiled=True)
    all_counts = lax.all_gather(counts, ("patch", "fsdp"), axis=0, tiled=False)
    counts_here = lax.dynamic_index_in_dim(
        all_counts.reshape(patches, groups, patches), lax.axis_index("patch"), 2, keepdims=False
    ).T
    live = (jnp.arange(capacity, dtype=jnp.int32)[None, None, :] < counts_here[:, :, None]).reshape(-1, 1)
    live = jnp.broadcast_to(live.astype(jnp.bfloat16), (live.shape[0], head_width))
    obs_rows = packed.reshape(patches * capacity, observed.shape[1])
    obs_all = lax.all_gather(obs_rows, "fsdp", axis=0, tiled=True)
    queries = jnp.dot(all_grid, query_weight, preferred_element_type=jnp.float32).astype(jnp.bfloat16)
    own_columns = lambda array: lax.dynamic_slice_in_dim(array, place * columns, columns, 1)
    assimilated_columns = attend(
        queries,
        obs_all,
        live,
        own_columns(key_weight),
        own_columns(value_weight),
        own_columns(all_grid),
        head_width,
    )
    assimilated = lax.all_gather(assimilated_columns, "fsdp", axis=1, tiled=True)
    all_values = assimilated.astype(jnp.float32)
    all_removed = all_values - jnp.mean(all_values, axis=-1, keepdims=True)
    all_inverse = lax.rsqrt(jnp.mean(all_removed * all_removed, axis=-1, keepdims=True) + eps)
    all_normed = (all_removed * all_inverse * gain).astype(jnp.bfloat16)
    own_rows = lambda array: lax.dynamic_slice_in_dim(array, place * token_count, token_count, 0)
    values32 = own_rows(assimilated).astype(jnp.float32)
    inverse_stddev = own_rows(all_inverse)
    standardized_input = (values32 - jnp.mean(values32, axis=-1, keepdims=True)) * inverse_stddev
    pre = jnp.dot(all_normed, up_weight, preferred_element_type=jnp.float32)
    hidden = gelu_tanh(pre).astype(jnp.bfloat16)
    all_cot = lax.all_gather(cotangent, "fsdp", axis=0, tiled=True)
    half = hidden.shape[1] // 2
    part = lambda rows, cols: lax.dot_general(
        rows, cols, (((0,), (0,)), ((), ())), preferred_element_type=jnp.float32
    ).astype(jnp.bfloat16)
    down_low = scatter_line_first(part(all_cot, hidden[:, :half]), patches)
    down_high = scatter_pair_first(part(all_cot, hidden[:, half:]), patches)
    branch = lax.psum_scatter(
        jnp.dot(hidden, down_weight, preferred_element_type=jnp.float32).astype(jnp.bfloat16),
        "fsdp",
        scatter_dimension=0,
        tiled=True,
    ).astype(jnp.float32)
    layer_output = (values32 + branch).astype(jnp.bfloat16)
    back_hidden = lax.dot_general(
        all_cot, down_weight, (((1,), (1,)), ((), ())), preferred_element_type=jnp.float32
    )
    slope = jax.vjp(gelu_tanh, pre)[1](back_hidden)[0]
    pre_grad = slope.astype(jnp.bfloat16)
    up_low = scatter_pair_first(part(all_normed, pre_grad[:, :half]), patches)
    up_high = scatter_pair_first(part(all_normed, pre_grad[:, half:]), patches)
    normed_grad = lax.psum_scatter(
        lax.dot_general(
            pre_grad, up_weight, (((1,), (1,)), ((), ())), preferred_element_type=jnp.float32
        ).astype(jnp.bfloat16),
        "fsdp",
        scatter_dimension=0,
        tiled=True,
    ).astype(jnp.float32)
    gain_scaled = normed_grad * gain
    input_gradient = inverse_stddev * (
        gain_scaled
        - jnp.mean(gain_scaled, axis=-1, keepdims=True)
        - standardized_input * jnp.mean(gain_scaled * standardized_input, axis=-1, keepdims=True)
    )
    input_grad = (cotangent.astype(jnp.float32) + input_gradient).astype(jnp.bfloat16)
    up_grad = jnp.concatenate([up_low, up_high], axis=1)
    down_grad = jnp.concatenate([down_low, down_high], axis=1).T
    return (layer_output, input_grad, up_grad, down_grad)


def solution(mesh):
    in_specs = (
        P(("patch", "fsdp"), None),
        P(("patch", "fsdp"), None),
        P(("patch", "fsdp"), None),
        P(),
        P(None, "fsdp"),
        P(),
        P(),
        P(None, "fsdp"),
        P("fsdp", None),
        P(("patch", "fsdp"), None),
    )
    out_specs = (
        P(("patch", "fsdp"), None),
        P(("patch", "fsdp"), None),
        P("patch", "fsdp"),
        P("fsdp", "patch"),
    )
    return jax.shard_map(
        on_device, mesh=mesh, in_specs=in_specs, out_specs=out_specs, check_vma=False
    )
```

```python
import jax
import jax.numpy as jnp
from jax import lax
from jax.experimental import pallas as pl
from jax.experimental.layout import Layout, with_layout_constraint
from jax.experimental.pallas import tpu as pltpu
from jax.sharding import PartitionSpec as P

D = 2048
HEADS = 16
EMPTY = 8.0


eps = 1e-05


def gelu_tanh(values):
    return jax.nn.gelu(values, approximate=True)


def pack_rows(observed, route, patches, capacity):
    targets = route[:, 0]
    onehot = (targets[:, None] == jnp.arange(patches, dtype=jnp.int32)[None, :]).astype(jnp.int32)
    ranks = jnp.sum(onehot * (jnp.cumsum(onehot, axis=0) - 1), axis=1)
    slots = targets * capacity + ranks
    packed = (
        jnp.full((patches * capacity, observed.shape[1]), EMPTY, observed.dtype)
        .at[slots]
        .set(observed)
    )
    return packed.reshape(patches, capacity, observed.shape[1])


def attention_kernel(q_ref, obs_ref, wk_ref, wv_ref, grid_ref, out_ref, rows_ref, k_ref, v_ref, s_ref):
    keys, width = k_ref.shape
    block = min(1024, keys)
    rows = s_ref.shape[0]
    scale = 1.4426950408889634 / width**0.5

    @pl.when(pl.program_id(0) == 0)
    def _():
        for start in range(0, keys, block):
            piece = obs_ref[start : start + block, :]
            live = piece < 0.5 * (EMPTY + 6.0)
            rows_ref[start : start + block, :] = jnp.where(live, piece, jnp.zeros_like(piece))
            v_ref[start : start + block, width:] = jnp.where(
                live[:, :width], jnp.ones_like(piece[:, :width]), jnp.zeros_like(piece[:, :width])
            )

    for start in range(0, keys, block):
        piece = rows_ref[start : start + block, :]
        k_ref[start : start + block, :] = jnp.dot(
            piece, wk_ref[...], preferred_element_type=jnp.float32
        ).astype(jnp.bfloat16)
        v_ref[start : start + block, :width] = jnp.dot(
            piece, wv_ref[...], preferred_element_type=jnp.float32
        ).astype(jnp.bfloat16)

    @pl.loop(0, q_ref.shape[0] // rows)
    def _(index):
        here = pl.ds(pl.multiple_of(index * rows, rows), rows)
        queries = q_ref[here, :]
        peak = jnp.zeros((rows, 128), jnp.float32)
        for start in range(0, keys, block):
            scores = lax.dot_general(
                queries,
                k_ref[start : start + block, :],
                (((1,), (1,)), ((), ())),
                preferred_element_type=jnp.float32,
            )
            s_ref[:, start : start + block] = scores
            for lane in range(0, block, 128):
                peak = jnp.maximum(peak, scores[:, lane : lane + 128])
        rowmax = jnp.max(peak, axis=-1, keepdims=True)
        total = jnp.zeros((rows, 2 * width), jnp.float32)
        for start in range(0, keys, block):
            lifted = jnp.exp2((s_ref[:, start : start + block] - rowmax) * scale)
            total = total + jnp.dot(
                lifted.astype(jnp.bfloat16),
                v_ref[start : start + block, :],
                preferred_element_type=jnp.float32,
            )
        denominator = total[:, width:] + jnp.exp2(-rowmax * scale)
        attended = total[:, :width] / denominator
        out_ref[here, :] = (grid_ref[here, :].astype(jnp.float32) + attended).astype(jnp.bfloat16)


def attend(queries, obs_rows, key_cols, value_cols, grid_cols, head_width):
    tokens, columns = queries.shape
    keys, channels = obs_rows.shape
    rows = min(256, tokens)
    by_head = lambda length: pl.BlockSpec((length, head_width), lambda h: (0, h))
    whole = lambda shape: pl.BlockSpec(shape, lambda h: (0, 0))
    return pl.pallas_call(
        attention_kernel,
        grid=(columns // head_width,),
        in_specs=[
            by_head(tokens),
            whole((keys, channels)),
            by_head(channels),
            by_head(channels),
            by_head(tokens),
        ],
        out_specs=by_head(tokens),
        out_shape=jax.ShapeDtypeStruct((tokens, columns), jnp.bfloat16),
        scratch_shapes=[
            pltpu.VMEM((keys, channels), jnp.bfloat16),
            pltpu.VMEM((keys, head_width), jnp.bfloat16),
            pltpu.VMEM((keys, 2 * head_width), jnp.bfloat16),
            pltpu.VMEM((rows, keys), jnp.float32),
        ],
        compiler_params=pltpu.CompilerParams(vmem_limit_bytes=48 * 1024 * 1024),
        cost_estimate=pl.CostEstimate(
            flops=4 * tokens * keys * columns * 2, bytes_accessed=keys * channels * 4, transcendentals=tokens * keys * 4
        ),
    )(queries, obs_rows, key_cols, value_cols, grid_cols)


def pick(parts, index):
    return lax.dynamic_index_in_dim(parts, index, 0, keepdims=False)


def add(first, second):
    return (first.astype(jnp.float32) + second.astype(jnp.float32)).astype(jnp.bfloat16)


def line_scatter(parts, place, length):
    right = left = None
    for step in range(length - 1):
        send = pick(parts, jnp.clip(length - 1 - step + place, 0, length - 1))
        right = lax.ppermute(
            send if right is None else add(send, right),
            "patch",
            [(2 * a + y, 2 * a + 2 + y) for a in range(step + 1) for y in range(2)],
        )
        send = pick(parts, jnp.clip(step - (length - 1) + place, 0, length - 1))
        left = lax.ppermute(
            send if left is None else add(send, left),
            "patch",
            [(2 * a + y, 2 * a - 2 + y) for a in range(length - 1 - step, length) for y in range(2)],
        )
    total = pick(parts, place).astype(jnp.float32)
    return total if right is None else total + right.astype(jnp.float32) + left.astype(jnp.float32)


def swap_pairs(patches):
    return [(p, p ^ 1) for p in range(patches)]


def scatter_pair_first(partial, patches):
    length = patches // 2
    patch = lax.axis_index("patch")
    place, side = patch // 2, patch % 2
    blocks = partial.reshape(length, 2, -1, partial.shape[1])
    mine = lax.dynamic_index_in_dim(blocks, side, 1, keepdims=False)
    theirs = lax.dynamic_index_in_dim(blocks, 1 - side, 1, keepdims=False)
    return line_scatter(add(mine, lax.ppermute(theirs, "patch", swap_pairs(patches))), place, length)


def scatter_line_first(partial, patches):
    length = patches // 2
    patch = lax.axis_index("patch")
    place, side = patch // 2, patch % 2
    blocks = partial.reshape(length, 2, -1, partial.shape[1])
    pair = line_scatter(blocks, place, length)
    got = lax.ppermute(pick(pair, 1 - side).astype(jnp.bfloat16), "patch", swap_pairs(patches))
    return pick(pair, side) + got.astype(jnp.float32)


def on_device(
    observed,
    route,
    grid,
    gain,
    query_weight,
    key_weight,
    value_weight,
    up_weight,
    down_weight,
    cotangent,
):
    patches = lax.axis_size("patch")
    groups = lax.axis_size("fsdp")
    place = lax.axis_index("fsdp")
    token_count = grid.shape[0]
    head_width = D // HEADS
    columns = query_weight.shape[1]
    capacity = 2 * observed.shape[0] // patches
    all_grid = lax.all_gather(grid, "fsdp", axis=0, tiled=True)
    packed = pack_rows(observed, route, patches, capacity)
    packed = lax.all_to_all(packed, "patch", split_axis=0, concat_axis=0, tiled=True)
    obs_rows = packed.reshape(patches * capacity, observed.shape[1])
    obs_all = lax.all_gather(obs_rows, "fsdp", axis=0, tiled=True)
    queries = jnp.dot(all_grid, query_weight, preferred_element_type=jnp.float32).astype(jnp.bfloat16)
    own_columns = lambda array: lax.dynamic_slice_in_dim(array, place * columns, columns, 1)
    assimilated_columns = attend(
        queries,
        obs_all,
        own_columns(key_weight),
        own_columns(value_weight),
        own_columns(all_grid),
        head_width,
    )
    assimilated = lax.all_gather(assimilated_columns, "fsdp", axis=1, tiled=True)
    all_values = assimilated.astype(jnp.float32)
    all_removed = all_values - jnp.mean(all_values, axis=-1, keepdims=True)
    all_inverse = lax.rsqrt(jnp.mean(all_removed * all_removed, axis=-1, keepdims=True) + eps)
    all_normed = (all_removed * all_inverse * gain).astype(jnp.bfloat16)
    own_rows = lambda array: lax.dynamic_slice_in_dim(array, place * token_count, token_count, 0)
    values32 = own_rows(assimilated).astype(jnp.float32)
    inverse_stddev = own_rows(all_inverse)
    standardized_input = (values32 - jnp.mean(values32, axis=-1, keepdims=True)) * inverse_stddev
    pre = jnp.dot(all_normed, up_weight, preferred_element_type=jnp.float32)
    hidden = gelu_tanh(pre).astype(jnp.bfloat16)
    all_cot = lax.all_gather(cotangent, "fsdp", axis=0, tiled=True)
    half = hidden.shape[1] // 2
    by_rows = lambda array: with_layout_constraint(array, Layout(major_to_minor=(0, 1)))
    part = lambda rows, cols: by_rows(
        lax.dot_general(
            rows, cols, (((0,), (0,)), ((), ())), preferred_element_type=jnp.float32
        ).astype(jnp.bfloat16)
    )
    down_low = scatter_line_first(part(all_cot, hidden[:, :half]), patches)
    down_high = scatter_pair_first(part(all_cot, hidden[:, half:]), patches)
    branch = lax.psum_scatter(
        jnp.dot(hidden, down_weight, preferred_element_type=jnp.float32).astype(jnp.bfloat16),
        "fsdp",
        scatter_dimension=0,
        tiled=True,
    ).astype(jnp.float32)
    layer_output = (values32 + branch).astype(jnp.bfloat16)
    back_hidden = lax.dot_general(
        all_cot, down_weight, (((1,), (1,)), ((), ())), preferred_element_type=jnp.float32
    )
    slope = jax.vjp(gelu_tanh, pre)[1](back_hidden)[0]
    pre_grad = slope.astype(jnp.bfloat16)
    up_low = scatter_pair_first(part(all_normed, pre_grad[:, :half]), patches)
    up_high = scatter_pair_first(part(all_normed, pre_grad[:, half:]), patches)
    normed_grad = lax.psum_scatter(
        lax.dot_general(
            pre_grad, up_weight, (((1,), (1,)), ((), ())), preferred_element_type=jnp.float32
        ).astype(jnp.bfloat16),
        "fsdp",
        scatter_dimension=0,
        tiled=True,
    ).astype(jnp.float32)
    gain_scaled = normed_grad * gain
    input_gradient = inverse_stddev * (
        gain_scaled
        - jnp.mean(gain_scaled, axis=-1, keepdims=True)
        - standardized_input * jnp.mean(gain_scaled * standardized_input, axis=-1, keepdims=True)
    )
    input_grad = (cotangent.astype(jnp.float32) + input_gradient).astype(jnp.bfloat16)
    up_grad = jnp.concatenate([up_low, up_high], axis=1)
    down_grad = by_rows(jnp.concatenate([down_low, down_high], axis=1)).T
    return (layer_output, input_grad, up_grad, down_grad)


def solution(mesh):
    in_specs = (
        P(("patch", "fsdp"), None),
        P(("patch", "fsdp"), None),
        P(("patch", "fsdp"), None),
        P(),
        P(None, "fsdp"),
        P(),
        P(),
        P(None, "fsdp"),
        P("fsdp", None),
        P(("patch", "fsdp"), None),
    )
    out_specs = (
        P(("patch", "fsdp"), None),
        P(("patch", "fsdp"), None),
        P("patch", "fsdp"),
        P("fsdp", "patch"),
    )
    return jax.shard_map(
        on_device, mesh=mesh, in_specs=in_specs, out_specs=out_specs, check_vma=False
    )
```

```python
import jax
import jax.numpy as jnp
from jax import lax
from jax.experimental import pallas as pl
from jax.experimental.layout import Layout, with_layout_constraint
from jax.experimental.pallas import tpu as pltpu
from jax.sharding import PartitionSpec as P

D = 2048
HEADS = 16
EMPTY = 8.0


eps = 1e-05


def gelu_tanh(values):
    return jax.nn.gelu(values, approximate=True)


def pack_rows(observed, route, patches, capacity):
    targets = route[:, 0]
    onehot = (targets[:, None] == jnp.arange(patches, dtype=jnp.int32)[None, :]).astype(jnp.int32)
    ranks = jnp.sum(onehot * (jnp.cumsum(onehot, axis=0) - 1), axis=1)
    slots = targets * capacity + ranks
    packed = (
        jnp.full((patches * capacity, observed.shape[1]), EMPTY, observed.dtype)
        .at[slots]
        .set(observed)
    )
    return packed.reshape(patches, capacity, observed.shape[1])


def attention_kernel(q_ref, obs_ref, wk_ref, wv_ref, grid_ref, out_ref, rows_ref, k_ref, v_ref, s_ref):
    keys, width = k_ref.shape
    block = min(1024, keys)
    rows = s_ref.shape[0]
    scale = 1.4426950408889634 / width**0.5

    @pl.when(pl.program_id(0) == 0)
    def _():
        for start in range(0, keys, block):
            piece = obs_ref[start : start + block, :]
            live = piece < 0.5 * (EMPTY + 6.0)
            rows_ref[start : start + block, :] = jnp.where(live, piece, jnp.zeros_like(piece))
            v_ref[start : start + block, width:] = jnp.where(
                live[:, :width], jnp.ones_like(piece[:, :width]), jnp.zeros_like(piece[:, :width])
            )

    for start in range(0, keys, block):
        piece = rows_ref[start : start + block, :]
        k_ref[start : start + block, :] = jnp.dot(
            piece, wk_ref[...], preferred_element_type=jnp.float32
        ).astype(jnp.bfloat16)
        v_ref[start : start + block, :width] = jnp.dot(
            piece, wv_ref[...], preferred_element_type=jnp.float32
        ).astype(jnp.bfloat16)

    @pl.loop(0, q_ref.shape[0] // rows)
    def _(index):
        here = pl.ds(pl.multiple_of(index * rows, rows), rows)
        queries = q_ref[here, :]
        peak = jnp.zeros((rows, 128), jnp.float32)
        for start in range(0, keys, block):
            scores = lax.dot_general(
                queries,
                k_ref[start : start + block, :],
                (((1,), (1,)), ((), ())),
                preferred_element_type=jnp.float32,
            )
            s_ref[:, start : start + block] = scores
            for lane in range(0, block, 128):
                peak = jnp.maximum(peak, scores[:, lane : lane + 128])
        rowmax = jnp.max(peak, axis=-1, keepdims=True)
        total = jnp.zeros((rows, 2 * width), jnp.float32)
        for start in range(0, keys, block):
            lifted = jnp.exp2((s_ref[:, start : start + block] - rowmax) * scale)
            total = total + jnp.dot(
                lifted.astype(jnp.bfloat16),
                v_ref[start : start + block, :],
                preferred_element_type=jnp.float32,
            )
        denominator = total[:, width:] + jnp.exp2(-rowmax * scale)
        attended = total[:, :width] / denominator
        out_ref[here, :] = (grid_ref[here, :].astype(jnp.float32) + attended).astype(jnp.bfloat16)


def attend(queries, obs_rows, key_cols, value_cols, grid_cols, head_width):
    tokens, columns = queries.shape
    keys, channels = obs_rows.shape
    rows = min(256, tokens)
    by_head = lambda length: pl.BlockSpec((length, head_width), lambda h: (0, h))
    whole = lambda shape: pl.BlockSpec(shape, lambda h: (0, 0))
    return pl.pallas_call(
        attention_kernel,
        grid=(columns // head_width,),
        in_specs=[
            by_head(tokens),
            whole((keys, channels)),
            by_head(channels),
            by_head(channels),
            by_head(tokens),
        ],
        out_specs=by_head(tokens),
        out_shape=jax.ShapeDtypeStruct((tokens, columns), jnp.bfloat16),
        scratch_shapes=[
            pltpu.VMEM((keys, channels), jnp.bfloat16),
            pltpu.VMEM((keys, head_width), jnp.bfloat16),
            pltpu.VMEM((keys, 2 * head_width), jnp.bfloat16),
            pltpu.VMEM((rows, keys), jnp.float32),
        ],
        compiler_params=pltpu.CompilerParams(vmem_limit_bytes=48 * 1024 * 1024),
        cost_estimate=pl.CostEstimate(
            flops=4 * tokens * keys * columns * 2, bytes_accessed=keys * channels * 4, transcendentals=tokens * keys * 4
        ),
    )(queries, obs_rows, key_cols, value_cols, grid_cols)


def pick(parts, index):
    return lax.dynamic_index_in_dim(parts, index, 0, keepdims=False)


def add(first, second):
    return (first.astype(jnp.float32) + second.astype(jnp.float32)).astype(jnp.bfloat16)


def line_scatter(parts, place, length):
    total = pick(parts, place).astype(jnp.float32)
    received = [
        lax.ppermute(
            pick(parts, lax.rem(place + shift, length)),
            "patch",
            [(2 * a + y, 2 * ((a + shift) % length) + y) for a in range(length) for y in range(2)],
        )
        for shift in range(1, length)
    ]
    for block in received:
        total = total + block.astype(jnp.float32)
    return total


def swap_pairs(patches):
    return [(p, p ^ 1) for p in range(patches)]


def scatter_pair_first(partial, patches):
    length = patches // 2
    patch = lax.axis_index("patch")
    place, side = patch // 2, patch % 2
    blocks = partial.reshape(length, 2, -1, partial.shape[1])
    mine = lax.dynamic_index_in_dim(blocks, side, 1, keepdims=False)
    theirs = lax.dynamic_index_in_dim(blocks, 1 - side, 1, keepdims=False)
    return line_scatter(add(mine, lax.ppermute(theirs, "patch", swap_pairs(patches))), place, length)


def scatter_line_first(partial, patches):
    length = patches // 2
    patch = lax.axis_index("patch")
    place, side = patch // 2, patch % 2
    blocks = partial.reshape(length, 2, -1, partial.shape[1])
    pair = line_scatter(blocks, place, length)
    got = lax.ppermute(pick(pair, 1 - side).astype(jnp.bfloat16), "patch", swap_pairs(patches))
    return pick(pair, side) + got.astype(jnp.float32)


def on_device(
    observed,
    route,
    grid,
    gain,
    query_weight,
    key_weight,
    value_weight,
    up_weight,
    down_weight,
    cotangent,
):
    patches = lax.axis_size("patch")
    groups = lax.axis_size("fsdp")
    place = lax.axis_index("fsdp")
    token_count = grid.shape[0]
    head_width = D // HEADS
    columns = query_weight.shape[1]
    capacity = 2 * observed.shape[0] // patches
    all_grid = lax.all_gather(grid, "fsdp", axis=0, tiled=True)
    packed = pack_rows(observed, route, patches, capacity)
    packed = lax.all_to_all(packed, "patch", split_axis=0, concat_axis=0, tiled=True)
    obs_rows = packed.reshape(patches * capacity, observed.shape[1])
    obs_all = lax.all_gather(obs_rows, "fsdp", axis=0, tiled=True)
    queries = jnp.dot(all_grid, query_weight, preferred_element_type=jnp.float32).astype(jnp.bfloat16)
    own_columns = lambda array: lax.dynamic_slice_in_dim(array, place * columns, columns, 1)
    assimilated_columns = attend(
        queries,
        obs_all,
        own_columns(key_weight),
        own_columns(value_weight),
        own_columns(all_grid),
        head_width,
    )
    assimilated = lax.all_gather(assimilated_columns, "fsdp", axis=1, tiled=True)
    all_values = assimilated.astype(jnp.float32)
    all_removed = all_values - jnp.mean(all_values, axis=-1, keepdims=True)
    all_inverse = lax.rsqrt(jnp.mean(all_removed * all_removed, axis=-1, keepdims=True) + eps)
    all_normed = (all_removed * all_inverse * gain).astype(jnp.bfloat16)
    own_rows = lambda array: lax.dynamic_slice_in_dim(array, place * token_count, token_count, 0)
    values32 = own_rows(assimilated).astype(jnp.float32)
    inverse_stddev = own_rows(all_inverse)
    standardized_input = (values32 - jnp.mean(values32, axis=-1, keepdims=True)) * inverse_stddev
    pre = jnp.dot(all_normed, up_weight, preferred_element_type=jnp.float32)
    hidden = gelu_tanh(pre).astype(jnp.bfloat16)
    all_cot = lax.all_gather(cotangent, "fsdp", axis=0, tiled=True)
    half = hidden.shape[1] // 2
    by_rows = lambda array: with_layout_constraint(array, Layout(major_to_minor=(0, 1)))
    part = lambda rows, cols: by_rows(
        lax.dot_general(
            rows, cols, (((0,), (0,)), ((), ())), preferred_element_type=jnp.float32
        ).astype(jnp.bfloat16)
    )
    down_low = scatter_line_first(part(all_cot, hidden[:, :half]), patches)
    down_high = scatter_pair_first(part(all_cot, hidden[:, half:]), patches)
    branch = lax.psum_scatter(
        jnp.dot(hidden, down_weight, preferred_element_type=jnp.float32).astype(jnp.bfloat16),
        "fsdp",
        scatter_dimension=0,
        tiled=True,
    ).astype(jnp.float32)
    layer_output = (values32 + branch).astype(jnp.bfloat16)
    back_hidden = lax.dot_general(
        all_cot, down_weight, (((1,), (1,)), ((), ())), preferred_element_type=jnp.float32
    )
    slope = jax.vjp(gelu_tanh, pre)[1](back_hidden)[0]
    pre_grad = slope.astype(jnp.bfloat16)
    up_low = scatter_pair_first(part(all_normed, pre_grad[:, :half]), patches)
    up_high = scatter_pair_first(part(all_normed, pre_grad[:, half:]), patches)
    normed_grad = lax.psum_scatter(
        lax.dot_general(
            pre_grad, up_weight, (((1,), (1,)), ((), ())), preferred_element_type=jnp.float32
        ).astype(jnp.bfloat16),
        "fsdp",
        scatter_dimension=0,
        tiled=True,
    ).astype(jnp.float32)
    gain_scaled = normed_grad * gain
    input_gradient = inverse_stddev * (
        gain_scaled
        - jnp.mean(gain_scaled, axis=-1, keepdims=True)
        - standardized_input * jnp.mean(gain_scaled * standardized_input, axis=-1, keepdims=True)
    )
    input_grad = (cotangent.astype(jnp.float32) + input_gradient).astype(jnp.bfloat16)
    up_grad = jnp.concatenate([up_low, up_high], axis=1)
    down_grad = by_rows(jnp.concatenate([down_low, down_high], axis=1)).T
    return (layer_output, input_grad, up_grad, down_grad)


def solution(mesh):
    in_specs = (
        P(("patch", "fsdp"), None),
        P(("patch", "fsdp"), None),
        P(("patch", "fsdp"), None),
        P(),
        P(None, "fsdp"),
        P(),
        P(),
        P(None, "fsdp"),
        P("fsdp", None),
        P(("patch", "fsdp"), None),
    )
    out_specs = (
        P(("patch", "fsdp"), None),
        P(("patch", "fsdp"), None),
        P("patch", "fsdp"),
        P("fsdp", "patch"),
    )
    return jax.shard_map(
        on_device, mesh=mesh, in_specs=in_specs, out_specs=out_specs, check_vma=False
    )
```

```python
import jax
import jax.numpy as jnp
from jax import lax
from jax.experimental import pallas as pl
from jax.experimental.layout import Layout, with_layout_constraint
from jax.experimental.pallas import tpu as pltpu
from jax.sharding import PartitionSpec as P

D = 2048
HEADS = 16
EMPTY = 8.0


eps = 1e-05


def gelu_tanh(values):
    return jax.nn.gelu(values, approximate=True)


def pack_rows(observed, route, patches, capacity):
    targets = route[:, 0]
    onehot = (targets[:, None] == jnp.arange(patches, dtype=jnp.int32)[None, :]).astype(jnp.int32)
    ranks = jnp.sum(onehot * (jnp.cumsum(onehot, axis=0) - 1), axis=1)
    slots = targets * capacity + ranks
    packed = (
        jnp.full((patches * capacity, observed.shape[1]), EMPTY, observed.dtype)
        .at[slots]
        .set(observed)
    )
    return packed.reshape(patches, capacity, observed.shape[1])


def attention_kernel(q_ref, obs_ref, wk_ref, wv_ref, grid_ref, out_ref, rows_ref, k_ref, v_ref, s_ref):
    keys, width = k_ref.shape
    block = min(1024, keys)
    rows = s_ref.shape[0]
    scale = 1.4426950408889634 / width**0.5

    @pl.when(pl.program_id(0) == 0)
    def _():
        for start in range(0, keys, block):
            piece = obs_ref[start : start + block, :]
            live = piece < 0.5 * (EMPTY + 6.0)
            rows_ref[start : start + block, :] = jnp.where(live, piece, jnp.zeros_like(piece))
            v_ref[start : start + block, width:] = jnp.where(
                live[:, :width], jnp.ones_like(piece[:, :width]), jnp.zeros_like(piece[:, :width])
            )

    for start in range(0, keys, block):
        piece = rows_ref[start : start + block, :]
        k_ref[start : start + block, :] = jnp.dot(
            piece, wk_ref[...], preferred_element_type=jnp.float32
        ).astype(jnp.bfloat16)
        v_ref[start : start + block, :width] = jnp.dot(
            piece, wv_ref[...], preferred_element_type=jnp.float32
        ).astype(jnp.bfloat16)

    @pl.loop(0, q_ref.shape[0] // rows)
    def _(index):
        here = pl.ds(pl.multiple_of(index * rows, rows), rows)
        queries = q_ref[here, :]
        peak = jnp.zeros((rows, 128), jnp.float32)
        for start in range(0, keys, block):
            scores = lax.dot_general(
                queries,
                k_ref[start : start + block, :],
                (((1,), (1,)), ((), ())),
                preferred_element_type=jnp.float32,
            )
            s_ref[:, start : start + block] = scores
            for lane in range(0, block, 128):
                peak = jnp.maximum(peak, scores[:, lane : lane + 128])
        rowmax = jnp.max(peak, axis=-1, keepdims=True)
        total = jnp.zeros((rows, 2 * width), jnp.float32)
        for start in range(0, keys, block):
            lifted = jnp.exp2((s_ref[:, start : start + block] - rowmax) * scale)
            total = total + jnp.dot(
                lifted.astype(jnp.bfloat16),
                v_ref[start : start + block, :],
                preferred_element_type=jnp.float32,
            )
        denominator = total[:, width:] + jnp.exp2(-rowmax * scale)
        attended = total[:, :width] / denominator
        out_ref[here, :] = (grid_ref[here, :].astype(jnp.float32) + attended).astype(jnp.bfloat16)


def attend(queries, obs_rows, key_cols, value_cols, grid_cols, head_width):
    tokens, columns = queries.shape
    keys, channels = obs_rows.shape
    rows = min(256, tokens)
    by_head = lambda length: pl.BlockSpec((length, head_width), lambda h: (0, h))
    whole = lambda shape: pl.BlockSpec(shape, lambda h: (0, 0))
    return pl.pallas_call(
        attention_kernel,
        grid=(columns // head_width,),
        in_specs=[
            by_head(tokens),
            whole((keys, channels)),
            by_head(channels),
            by_head(channels),
            by_head(tokens),
        ],
        out_specs=by_head(tokens),
        out_shape=jax.ShapeDtypeStruct((tokens, columns), jnp.bfloat16),
        scratch_shapes=[
            pltpu.VMEM((keys, channels), jnp.bfloat16),
            pltpu.VMEM((keys, head_width), jnp.bfloat16),
            pltpu.VMEM((keys, 2 * head_width), jnp.bfloat16),
            pltpu.VMEM((rows, keys), jnp.float32),
        ],
        compiler_params=pltpu.CompilerParams(vmem_limit_bytes=48 * 1024 * 1024),
        cost_estimate=pl.CostEstimate(
            flops=4 * tokens * keys * columns * 2, bytes_accessed=keys * channels * 4, transcendentals=tokens * keys * 4
        ),
    )(queries, obs_rows, key_cols, value_cols, grid_cols)


def pick(parts, index):
    return lax.dynamic_index_in_dim(parts, index, 0, keepdims=False)


def add(first, second):
    return (first.astype(jnp.float32) + second.astype(jnp.float32)).astype(jnp.bfloat16)


def line_scatter(parts, place, length):
    total = pick(parts, place).astype(jnp.float32)
    received = [
        lax.ppermute(
            pick(parts, lax.rem(place + shift, length)),
            "patch",
            [(2 * a + y, 2 * ((a + shift) % length) + y) for a in range(length) for y in range(2)],
        )
        for shift in range(1, length)
    ]
    for block in received:
        total = total + block.astype(jnp.float32)
    return total


def swap_pairs(patches):
    return [(p, p ^ 1) for p in range(patches)]


def scatter_pair_first(partial, patches):
    length = patches // 2
    patch = lax.axis_index("patch")
    place, side = patch // 2, patch % 2
    blocks = partial.reshape(length, 2, -1, partial.shape[1])
    mine = lax.dynamic_index_in_dim(blocks, side, 1, keepdims=False)
    theirs = lax.dynamic_index_in_dim(blocks, 1 - side, 1, keepdims=False)
    return line_scatter(add(mine, lax.ppermute(theirs, "patch", swap_pairs(patches))), place, length)


def scatter_line_first(partial, patches):
    length = patches // 2
    patch = lax.axis_index("patch")
    place, side = patch // 2, patch % 2
    blocks = partial.reshape(length, 2, -1, partial.shape[1])
    pair = line_scatter(blocks, place, length)
    got = lax.ppermute(pick(pair, 1 - side).astype(jnp.bfloat16), "patch", swap_pairs(patches))
    return pick(pair, side) + got.astype(jnp.float32)


def on_device(
    observed,
    route,
    grid,
    gain,
    query_weight,
    key_weight,
    value_weight,
    up_weight,
    down_weight,
    cotangent,
):
    patches = lax.axis_size("patch")
    groups = lax.axis_size("fsdp")
    place = lax.axis_index("fsdp")
    token_count = grid.shape[0]
    head_width = D // HEADS
    columns = query_weight.shape[1]
    capacity = 2 * observed.shape[0] // patches
    all_grid = lax.all_gather(grid, "fsdp", axis=0, tiled=True)
    packed = pack_rows(observed, route, patches, capacity)
    packed = lax.all_to_all(packed, "patch", split_axis=0, concat_axis=0, tiled=True)
    obs_rows = packed.reshape(patches * capacity, observed.shape[1])
    obs_all = lax.all_gather(obs_rows, "fsdp", axis=0, tiled=True)
    queries = jnp.dot(all_grid, query_weight, preferred_element_type=jnp.float32).astype(jnp.bfloat16)
    own_columns = lambda array: lax.dynamic_slice_in_dim(array, place * columns, columns, 1)
    assimilated_columns = attend(
        queries,
        obs_all,
        own_columns(key_weight),
        own_columns(value_weight),
        own_columns(all_grid),
        head_width,
    )
    assimilated = lax.all_gather(assimilated_columns, "fsdp", axis=1, tiled=True)
    all_values = assimilated.astype(jnp.float32)
    all_removed = all_values - jnp.mean(all_values, axis=-1, keepdims=True)
    all_inverse = lax.rsqrt(jnp.mean(all_removed * all_removed, axis=-1, keepdims=True) + eps)
    all_normed = (all_removed * all_inverse * gain).astype(jnp.bfloat16)
    own_rows = lambda array: lax.dynamic_slice_in_dim(array, place * token_count, token_count, 0)
    values32 = own_rows(assimilated).astype(jnp.float32)
    inverse_stddev = own_rows(all_inverse)
    standardized_input = (values32 - jnp.mean(values32, axis=-1, keepdims=True)) * inverse_stddev
    pre = jnp.dot(all_normed, up_weight, preferred_element_type=jnp.float32)
    hidden = gelu_tanh(pre).astype(jnp.bfloat16)
    all_cot = lax.all_gather(cotangent, "fsdp", axis=0, tiled=True)
    half = hidden.shape[1] // 2
    by_rows = lambda array: with_layout_constraint(array, Layout(major_to_minor=(0, 1)))
    part = lambda rows, cols: by_rows(
        lax.dot_general(
            rows, cols, (((0,), (0,)), ((), ())), preferred_element_type=jnp.float32
        ).astype(jnp.bfloat16)
    )
    quarter = half // 2
    down_first = scatter_line_first(part(all_cot, hidden[:, :quarter]), patches)
    down_low = scatter_pair_first(part(all_cot, hidden[:, quarter:half]), patches)
    down_high = scatter_pair_first(part(all_cot, hidden[:, half:]), patches)
    branch = lax.psum_scatter(
        jnp.dot(hidden, down_weight, preferred_element_type=jnp.float32).astype(jnp.bfloat16),
        "fsdp",
        scatter_dimension=0,
        tiled=True,
    ).astype(jnp.float32)
    layer_output = (values32 + branch).astype(jnp.bfloat16)
    back_hidden = lax.dot_general(
        all_cot, down_weight, (((1,), (1,)), ((), ())), preferred_element_type=jnp.float32
    )
    slope = jax.vjp(gelu_tanh, pre)[1](back_hidden)[0]
    pre_grad = slope.astype(jnp.bfloat16)
    up_low = scatter_pair_first(part(all_normed, pre_grad[:, :half]), patches)
    up_high = scatter_pair_first(part(all_normed, pre_grad[:, half:]), patches)
    normed_grad = lax.psum_scatter(
        lax.dot_general(
            pre_grad, up_weight, (((1,), (1,)), ((), ())), preferred_element_type=jnp.float32
        ).astype(jnp.bfloat16),
        "fsdp",
        scatter_dimension=0,
        tiled=True,
    ).astype(jnp.float32)
    gain_scaled = normed_grad * gain
    input_gradient = inverse_stddev * (
        gain_scaled
        - jnp.mean(gain_scaled, axis=-1, keepdims=True)
        - standardized_input * jnp.mean(gain_scaled * standardized_input, axis=-1, keepdims=True)
    )
    input_grad = (cotangent.astype(jnp.float32) + input_gradient).astype(jnp.bfloat16)
    up_grad = jnp.concatenate([up_low, up_high], axis=1)
    down_grad = by_rows(jnp.concatenate([down_first, down_low, down_high], axis=1)).T
    return (layer_output, input_grad, up_grad, down_grad)


def solution(mesh):
    in_specs = (
        P(("patch", "fsdp"), None),
        P(("patch", "fsdp"), None),
        P(("patch", "fsdp"), None),
        P(),
        P(None, "fsdp"),
        P(),
        P(),
        P(None, "fsdp"),
        P("fsdp", None),
        P(("patch", "fsdp"), None),
    )
    out_specs = (
        P(("patch", "fsdp"), None),
        P(("patch", "fsdp"), None),
        P("patch", "fsdp"),
        P("fsdp", "patch"),
    )
    return jax.shard_map(
        on_device, mesh=mesh, in_specs=in_specs, out_specs=out_specs, check_vma=False
    )
```
